512 devices in a mesh: trade: 64 (over x, y, core), scen: 8 (over z).
Axes of the slice: x: 4, y: 8, z: 8, core: 2. Of those that a mesh axis runs over, the one named last changes fastest.
Arguments:
- draws: bfloat16 [8, 512, 4096], P('scen', 'trade'), may hold values from -5 to 5
- loadings: bfloat16 [4096, 4096], P('trade'), may hold values from -0.09375 to 0.09375
- base_yield: float32 [4096], P('trade'), may hold values from 0.005 to 0.06
- cashflows: bfloat16 [64, 131072], P(None, 'trade'), may hold values from -0.3125 to 0.3125
- netting_id: int32 [131072], P('trade'), may hold values from 0 to 1023
- live_trades: int32 [64], P('trade'), may hold values from 1 to 2048, 78643 in all
- dist_prev: float32 [1024, 4096], P('trade', 'scen'), may hold values from -0.15 to 0.6
- shock: float32 [1024, 4096], P('trade', 'scen'), may hold values from -5 to 5
- vol: float32 [1024], P('trade'), may hold values from 0.2 to 0.8
Outputs:
- net_value: float32 [1024, 4096], P('trade', 'scen')
- expected_loss: float32 [1024], P('trade')
The draws below stay inside these ranges and needn't reach their ends.
All inputs are finite; a program needn't handle non-finite values. No bound on the sum of `live_trades` on one device may be relied on, other than what follows from the above.
Results may differ from the reference program's by a relative error of at most 0.003.
Values may be sent and summed in bfloat16 or wider, within the bound.
No kernel may reach another device: no remote copies, remote signals or barrier semaphores. Data moves between devices by JAX's collectives and lax.ppermute only.
A program may use at most 64 MiB of HBM per device.

```python
import math
import jax
import jax.numpy as jnp
import numpy as np
from jax import lax

K = 4096
TRADE_DEV = 2048
PILLARS = 64
PRICE_DEV = 512
S = 4096
TRADES = 131072
NS = 1024
N_TRADE = 64
N_SCEN = 8


def place_ends(result, key, least, high):
    extent = result.shape
    spot = [jax.random.randint(jax.random.fold_in(key, axis), (), 0, extent[axis]) for axis in range(len(extent))]
    result = result.at[tuple(spot)].set(least)
    longest = extent.index(max(extent))
    spot[longest] = (spot[longest] + 1) % extent[longest]
    return result.at[tuple(spot)].set(high)


def steps_of(stream_key, extent, cuts, smallest, high):
    loudness = 1.0
    for position, shards_of in cuts:
        steps = jax.random.uniform(jax.random.fold_in(jax.random.fold_in(stream_key, 6), position), (shards_of,), jnp.float32, smallest / len(cuts), high / len(cuts))
        loudness = loudness * jnp.repeat(jnp.exp(steps), extent[position] // shards_of).reshape((-1,) + (1,) * (len(extent) - 1 - position))
    return loudness


def rank_table(count, skew):
    loads = [(1 << 20) // math.isqrt(standing ** skew) + 1 for standing in range(1, count + 1)]
    deviation = 1 + sum(loads) // (1 << 30)
    return np.cumsum(np.array([max(1, weight // deviation) for weight in loads]))


def skewed_ids(own_key, shape, number_of, lean):
    table = rank_table(number_of, lean)
    lot = jax.random.randint(jax.random.fold_in(own_key, 1), shape, 0, int(table[number_of - 1]))
    standing = jnp.searchsorted(jnp.asarray(table, jnp.int32), lot, side="right")
    return jax.random.permutation(jax.random.fold_in(own_key, 2), number_of)[standing].astype(jnp.int32)


def length_profile(number_of, total, bound, skew):
    portions = [(1 << 20) // math.isqrt(grade ** skew) + 1 for grade in range(2, number_of + 1)]
    rest, given = total - bound - (number_of - 1), [1] * (number_of - 1)
    while rest > 0:
        free = [i for i in range(number_of - 1) if given[i] < bound]
        mass, budget = sum([portions[i] for i in free]), rest
        for i in free:
            more = min(bound - given[i], max(1, budget * portions[i] // mass), rest)
            given[i] = given[i] + more
            rest = rest - more
    return np.array([bound] + given)


def uneven_parts(key, number_of, total, reach, skew):
    if number_of == 2:
        one = jax.random.randint(key, (), max(1, total - reach), min(reach, total - 1) + 1)
        return jnp.stack([one, total - one])
    sizes = jnp.asarray(length_profile(number_of, total, reach, skew), jnp.int32)
    twos = (number_of - 1) // 2
    donor, receiver = sizes[1:1 + 2 * twos:2], sizes[2:2 + 2 * twos:2]
    margin = jnp.minimum(donor - 1, reach - receiver)
    shifted = jax.random.randint(jax.random.fold_in(key, 1), (twos,), 0, 1 << 20) % (margin + 1)
    sizes = sizes.at[1:1 + 2 * twos:2].set(donor - shifted).at[2:2 + 2 * twos:2].set(receiver + shifted)
    return sizes[jax.random.permutation(jax.random.fold_in(key, 2), number_of)]


def noise(key, shape, width, most, split=(), kind=jnp.bfloat16):
    entries = jax.random.normal(key, shape, jnp.float32) * width
    if len(split) > 0:
        entries = steps_of(key, shape, split, -0.22, 0.18) * entries
    return jnp.clip(entries, min=-most, max=most).astype(kind)


def setup_inputs(seed: int = 0) -> dict:
    key_list = jax.random.split(jax.random.key(seed), 10)
    draws = noise(key_list[0], (N_SCEN, PRICE_DEV, K), 1.0, 5.0, ((0, 8), (1, 64)))
    loadings = noise(key_list[1], (K, K), K ** -0.5, 0.09375, ((0, 64),))
    base_yield = jnp.clip(jnp.exp(math.log(0.06) - 2.4849066 * jax.random.uniform(key_list[2], (K,), jnp.float32) ** steps_of(key_list[2], (K,), ((0, 64),), -0.2, 0.2)), 0.005, 0.06)
    cashflows = noise(key_list[3], (PILLARS, TRADES), 0.02, 0.3125, ((1, 64),))
    netting_id = place_ends(skewed_ids(key_list[4], (TRADES,), NS, 1), jax.random.fold_in(key_list[4], 3), 0, NS - 1).astype(jnp.int32)
    live_trades = uneven_parts(key_list[5], N_TRADE, 3 * TRADE_DEV * N_TRADE // 5, TRADE_DEV, 2).astype(jnp.int32)
    dist_prev = jnp.clip(-0.15 + 0.75 * jax.random.uniform(key_list[6], (NS, S), jnp.float32) ** steps_of(key_list[6], (NS, S), ((0, 64), (1, 8)), -0.2, 0.2), -0.15, 0.6)
    shock = noise(key_list[7], (NS, S), 1.0, 5.0, ((0, 64), (1, 8)), jnp.float32)
    vol = jnp.clip(jnp.exp(math.log(0.8) - 1.3862944 * jax.random.uniform(key_list[8], (NS,), jnp.float32) ** steps_of(key_list[8], (NS,), ((0, 64),), -0.2, 0.2)), 0.2, 0.8)
    return dict(draws=draws, loadings=loadings, base_yield=base_yield, cashflows=cashflows, netting_id=netting_id, live_trades=live_trades, dist_prev=dist_prev, shock=shock, vol=vol)


def reference(draws, loadings, base_yield, cashflows, netting_id, live_trades, dist_prev, shock, vol):
    normals = draws.reshape(S, K)
    factors = lax.dot_general(normals, loadings, (((1,), (1,)), ((), ())), preferred_element_type=jnp.float32)
    tenors = (jnp.arange(K, dtype=jnp.int32) % PILLARS + 1).astype(jnp.float32) * (16.0 / PILLARS)
    discount = jnp.exp(-tenors[None, :] * (base_yield[None, :] + 0.02 * factors)).astype(jnp.bfloat16)

    def currency(totals, group):
        prices = lax.dynamic_slice_in_dim(discount, (group * PILLARS).astype(jnp.int32), PILLARS, 1)
        flows = lax.dynamic_slice_in_dim(cashflows, (group * TRADE_DEV).astype(jnp.int32), TRADE_DEV, 1)
        values = lax.dot_general(flows, prices, (((0,), (1,)), ((), ())), preferred_element_type=jnp.float32)
        alive = (jnp.arange(TRADE_DEV, dtype=jnp.int32) < live_trades[group]).astype(jnp.float32)
        set_ids = lax.dynamic_slice_in_dim(netting_id, (group * TRADE_DEV).astype(jnp.int32), TRADE_DEV, 0)
        return totals + jax.ops.segment_sum(values * alive[:, None], set_ids, NS), None

    net_value, _ = lax.scan(currency, jnp.zeros((NS, S), jnp.float32), jnp.arange(N_TRADE, dtype=jnp.int32))
    spread = vol[:, None]
    dist_now = dist_prev + (0.03 - 0.5 * spread * spread) + spread * shock
    crossing = jnp.exp(-2.0 * jnp.maximum(dist_prev, 0.0) * jnp.maximum(dist_now, 0.0) / (spread * spread))
    losses = jnp.maximum(net_value, 0.0) * crossing
    expected_loss = jnp.sum(losses, axis=1) / S
    return net_value, expected_loss
```

```python
import jax
import jax.numpy as jnp
from jax import lax
from jax.sharding import Mesh, PartitionSpec as P

TRADE = ("x", "y", "core")


def shift(value, axis, by):
    size = lax.axis_size(axis)
    return lax.ppermute(value, axis, [(i, (i + by) % size) for i in range(size)])


def everywhere(value, axis):
    size = lax.axis_size(axis)
    copies = jnp.broadcast_to(value[None], (size, *value.shape))
    return lax.all_to_all(copies, axis, 0, 0, tiled=True)


def netting_flows(cashflows, netting_id, live_count, set_total):
    trades = cashflows.shape[1]
    alive = jnp.arange(trades, dtype=jnp.int32) < live_count
    set_numbers = jnp.arange(set_total, dtype=jnp.int32)
    member = jnp.where(
        (netting_id[None, :] == set_numbers[:, None]) & alive[None, :], 1.0, 0.0
    ).astype(jnp.bfloat16)
    return lax.dot_general(
        cashflows, member, (((1,), (1,)), ((), ())), preferred_element_type=jnp.float32
    )


def body(draws, loadings, base_yield, cashflows, netting_id, live_trades, dist_prev, shock, vol):
    pillars = loadings.shape[0]
    owned, scen_rows = dist_prev.shape
    quarters = lax.axis_size("x")
    groups = quarters * lax.axis_size("y") * lax.axis_size("core")
    set_total = owned * groups
    part = scen_rows // quarters

    flows = netting_flows(cashflows, netting_id, live_trades[0], set_total)
    packed = jnp.concatenate(
        [flows, jnp.broadcast_to(base_yield[:, None], (pillars, 128))], axis=1
    )
    shifts = (1, -1, 2)
    loads = [loadings] + [shift(loadings, "x", by) for by in shifts]
    packs = [packed] + [shift(packed, "x", by) for by in shifts]

    mine = everywhere(draws[0], "y")
    other = shift(mine, "core", 1)
    first = lax.axis_index("core") == 0
    normals = jnp.where(
        first, jnp.stack([mine, other], axis=1), jnp.stack([other, mine], axis=1)
    ).reshape(part, -1)

    tenors = (jnp.arange(pillars, dtype=jnp.int32) + 1).astype(jnp.float32) * (16.0 / pillars)
    total = jnp.zeros((set_total, part), jnp.float32)
    for load, pack in zip(loads, packs):
        factors = lax.dot_general(
            load, normals, (((1,), (1,)), ((), ())), preferred_element_type=jnp.float32
        )
        yields = pack[:, set_total : set_total + 1]
        discount = jnp.exp(-tenors[:, None] * (yields + 0.02 * factors)).astype(jnp.bfloat16)
        flow = pack[:, :set_total]
        high = lax.reduce_precision(flow, 8, 7)
        for term in (high, flow - high):
            total = total + lax.dot_general(
                term.astype(jnp.bfloat16),
                discount,
                (((0,), (0,)), ((), ())),
                preferred_element_type=jnp.float32,
            )
    sent = lax.all_to_all(total.astype(jnp.bfloat16), TRADE, 0, 0, tiled=True)
    terms = sent.reshape(quarters, groups // quarters, owned, part).astype(jnp.float32)
    net_value = jnp.sum(terms, axis=1).transpose(1, 0, 2).reshape(owned, scen_rows)

    spread = vol[:, None]
    dist_now = dist_prev + (0.03 - 0.5 * spread * spread) + spread * shock
    crossing = jnp.exp(
        -2.0 * jnp.maximum(dist_prev, 0.0) * jnp.maximum(dist_now, 0.0) / (spread * spread)
    )
    losses = jnp.sum(jnp.maximum(net_value, 0.0) * crossing, axis=1)
    summed = jnp.sum(everywhere(losses, "scen").reshape(-1, owned), axis=0)
    expected_loss = summed / (scen_rows * lax.axis_size("scen"))
    return (net_value, expected_loss)


def solution(mesh):
    chips = Mesh(mesh.devices.reshape(4, 8, 2, 8), ("x", "y", "core", "scen"))
    in_specs = (
        P("scen", TRADE, None),
        P(TRADE, None),
        P(TRADE),
        P(None, TRADE),
        P(TRADE),
        P(TRADE),
        P(TRADE, "scen"),
        P(TRADE, "scen"),
        P(TRADE),
    )
    out_specs = (P(TRADE, "scen"), P(TRADE))
    return jax.shard_map(body, mesh=chips, in_specs=in_specs, out_specs=out_specs, check_vma=False)
```

```python
import jax
import jax.numpy as jnp
from jax import lax
from jax.experimental import pallas as pl
from jax.experimental.pallas import tpu as pltpu
from jax.sharding import Mesh, PartitionSpec as P

LANES = 128
LIMIT = 16
HINT = 5 * 10**9
PACK_LIMIT = 62
TRADE = ("x", "y", "core")


def shift(value, axis, by):
    size = lax.axis_size(axis)
    return lax.ppermute(value, axis, [(i, (i + by) % size) for i in range(size)])


def everywhere(value, axis):
    size = lax.axis_size(axis)
    copies = jnp.broadcast_to(value[None], (size, *value.shape))
    return lax.all_to_all(copies, axis, 0, 0, tiled=True)


def pack_kernel(
    live_ref, cash_hbm, id_ref, yield_ref, load_hbm, draw_hbm, out_hbm, copies_hbm,
    cash_ref, load_ref, draw_ref, fold_ref, sems
):
    pillars, trades = cash_ref.shape
    width = load_hbm.shape[1]
    rows = fold_ref.shape[0]
    set_total = width * rows // pillars
    cash_in = pltpu.make_async_copy(cash_hbm, cash_ref, sems.at[0])
    cash_in.start()
    draw_in = pltpu.make_async_copy(draw_hbm.at[0], draw_ref, sems.at[1])
    draw_in.start()
    load_in = pltpu.make_async_copy(load_hbm, load_ref.at[:, pl.ds(0, width)], sems.at[2])
    load_in.start()
    diagonal = lax.broadcasted_iota(jnp.int32, (pillars, pillars), 0) == lax.broadcasted_iota(
        jnp.int32, (pillars, pillars), 1
    )
    level = jnp.sum(jnp.where(diagonal, yield_ref[...], 0.0), axis=1, keepdims=True)
    upper = level.astype(jnp.bfloat16).astype(jnp.float32)
    middle = (level - upper).astype(jnp.bfloat16).astype(jnp.float32)
    lower = level - upper - middle
    lane = lax.broadcasted_iota(jnp.int32, (pillars, LANES), 1)
    terms = jnp.where(
        lane == 0, upper, jnp.where(lane == 1, middle, jnp.where(lane == 2, lower, 0.0))
    )
    load_ref[:, width:] = terms.astype(jnp.bfloat16)
    alive = lax.broadcasted_iota(jnp.int32, (1, trades), 1) < live_ref[0]
    owner = jnp.where(alive, id_ref[...], -1)
    fold_ref[:, width:] = jnp.zeros((rows, LANES), jnp.bfloat16)
    draw_in.wait()
    moves = [
        pltpu.make_async_copy(draw_ref, copies_hbm.at[i], sems.at[5 + i])
        for i in range(copies_hbm.shape[0])
    ]
    for move in moves:
        move.start()
    cash_in.wait()
    load_in.wait()
    load_out = pltpu.make_async_copy(load_ref, out_hbm.at[pl.ds(0, pillars)], sems.at[3])
    load_out.start()
    for first in range(0, set_total, 256):
        numbers = first + lax.broadcasted_iota(jnp.int32, (256, trades), 0)
        member = jnp.where(numbers == owner, 1.0, 0.0).astype(jnp.bfloat16)
        flows = lax.dot_general(
            cash_ref[...], member, (((1,), (1,)), ((), ())), preferred_element_type=jnp.float32
        ).astype(jnp.bfloat16)
        for i in range(pillars // rows):
            fold_ref[:, i * set_total + first : i * set_total + first + 256] = flows[
                i * rows : (i + 1) * rows
            ]
    fold_out = pltpu.make_async_copy(fold_ref, out_hbm.at[pl.ds(pillars, rows)], sems.at[4])
    fold_out.start()
    load_out.wait()
    fold_out.wait()
    for move in moves:
        move.wait()


def unfold_kernel(pack_ref, out_ref):
    pillars, set_total = out_ref.shape
    rows = pack_ref.shape[0] - pillars
    for i in range(pillars // rows):
        out_ref[i * rows : (i + 1) * rows, :] = pack_ref[
            pillars:, i * set_total : (i + 1) * set_total
        ]


def discounts(pack_ref, pillars, normals_ref):
    width = normals_ref.shape[1]
    factors = lax.dot_general(
        pack_ref[:pillars, :width],
        normals_ref[...],
        (((1,), (1,)), ((), ())),
        preferred_element_type=jnp.float32,
    )
    step = (lax.broadcasted_iota(jnp.int32, (pillars, 1), 0) + 1).astype(jnp.float32)
    level = jnp.sum(pack_ref[:pillars, width:].astype(jnp.float32), axis=1, keepdims=True)
    return jnp.exp(-step * (16.0 / pillars) * (level + 0.02 * factors)).astype(jnp.bfloat16)


def unfold(pack_ref, pillars, set_total):
    rows = pack_ref.shape[0] - pillars
    return jnp.concatenate(
        [
            pack_ref[pillars:, i * set_total : (i + 1) * set_total]
            for i in range(pillars // rows)
        ],
        axis=0,
    )


def first_kernel(
    core_ref, mine_ref, other_ref, own_ref, far_ref, early_ref, normals_ref, discount_ref, flow_ref
):
    pillars = early_ref.shape[0]
    set_total = early_ref.shape[1]
    rows = mine_ref.shape[1]

    def place(even_ref, odd_ref):
        for i in range(mine_ref.shape[0]):
            normals_ref[2 * i * rows : 2 * (i + 1) * rows, :] = jnp.concatenate(
                [even_ref[i], odd_ref[i]], axis=0
            )

    @pl.when(core_ref[0] == 0)
    def _():
        place(mine_ref, other_ref)

    @pl.when(core_ref[0] != 0)
    def _():
        place(other_ref, mine_ref)

    discount_ref[:pillars, :] = discounts(own_ref, pillars, normals_ref)
    discount_ref[pillars:, :] = discounts(far_ref, pillars, normals_ref)
    flow_ref[:pillars, :] = unfold(own_ref, pillars, set_total)
    flow_ref[pillars:, :] = early_ref[...]


def price_kernel(normals_ref, discount_ref, flow_ref, *refs):
    pack_refs, out_ref = refs[:-1], refs[-1]
    pillars = discount_ref.shape[0] // 2
    set_total = out_ref.shape[0]
    prices = [discount_ref[...]] + [discounts(ref, pillars, normals_ref) for ref in pack_refs]
    flows = [flow_ref[...]] + [unfold(ref, pillars, set_total) for ref in pack_refs]
    out_ref[...] = lax.dot_general(
        jnp.concatenate(flows, axis=0),
        jnp.concatenate(prices, axis=0),
        (((0,), (0,)), ((), ())),
        preferred_element_type=jnp.float32,
    ).astype(jnp.bfloat16)


def body(draws, loadings, base_yield, cashflows, netting_id, live_trades, dist_prev, shock, vol):
    pillars = loadings.shape[0]
    owned, scen_rows = dist_prev.shape
    quarters = lax.axis_size("x")
    groups = quarters * lax.axis_size("y") * lax.axis_size("core")
    set_total = owned * groups
    part = scen_rows // quarters
    width = loadings.shape[1]
    rows = pillars * set_total // width
    vmem = pl.BlockSpec(memory_space=pltpu.VMEM)
    hbm = pl.BlockSpec(memory_space=pltpu.HBM)
    smem = pl.BlockSpec(memory_space=pltpu.SMEM)
    params = pltpu.CompilerParams(vmem_limit_bytes=LIMIT << 20)

    packed, copies = pl.pallas_call(
        pack_kernel,
        out_shape=(
            jax.ShapeDtypeStruct((pillars + rows, width + LANES), jnp.bfloat16),
            jax.ShapeDtypeStruct((lax.axis_size("y"), *draws.shape[1:]), jnp.bfloat16),
        ),
        in_specs=[smem, hbm, vmem, vmem, hbm, hbm],
        out_specs=(hbm, hbm),
        scratch_shapes=[
            pltpu.VMEM(cashflows.shape, jnp.bfloat16),
            pltpu.VMEM((pillars, width + LANES), jnp.bfloat16),
            pltpu.VMEM(draws.shape[1:], jnp.bfloat16),
            pltpu.VMEM((rows, width + LANES), jnp.bfloat16),
            pltpu.SemaphoreType.DMA((5 + lax.axis_size("y"),)),
        ],
        compiler_params=pltpu.CompilerParams(vmem_limit_bytes=PACK_LIMIT << 20),
        name="pack",
    )(live_trades, cashflows, netting_id[None, :], base_yield[None, :], loadings, draws)
    packs = [shift(packed, "x", by) for by in (2, 1, -1)]
    mine = lax.all_to_all(copies, "y", 0, 0, tiled=True)
    early = pl.pallas_call(
        unfold_kernel,
        out_shape=jax.ShapeDtypeStruct((pillars, set_total), jnp.bfloat16),
        in_specs=[vmem],
        out_specs=vmem,
        compiler_params=params,
        cost_estimate=pl.CostEstimate(flops=HINT, bytes_accessed=0, transcendentals=0),
        name="unfold",
    )(packs[0])
    mine, early = lax.optimization_barrier((mine, early))
    other = shift(mine, "core", 1)
    normals, discount, flow = pl.pallas_call(
        first_kernel,
        out_shape=(
            jax.ShapeDtypeStruct((part, width), jnp.bfloat16),
            jax.ShapeDtypeStruct((2 * pillars, part), jnp.bfloat16),
            jax.ShapeDtypeStruct((2 * pillars, set_total), jnp.bfloat16),
        ),
        in_specs=[smem, vmem, vmem, vmem, vmem, vmem],
        out_specs=(vmem, vmem, vmem),
        compiler_params=params,
        name="first",
    )(lax.axis_index("core").astype(jnp.int32)[None], mine, other, packed, packs[0], early)
    total = pl.pallas_call(
        price_kernel,
        out_shape=jax.ShapeDtypeStruct((set_total, part), jnp.bfloat16),
        in_specs=[vmem] * 5,
        out_specs=vmem,
        compiler_params=params,
        name="price",
    )(normals, discount, flow, *packs[1:])
    sent = lax.all_to_all(total, TRADE, 0, 0, tiled=True)
    terms = sent.reshape(quarters, groups // quarters, owned, part).astype(jnp.float32)
    net_value = jnp.sum(terms, axis=1).transpose(1, 0, 2).reshape(owned, scen_rows)

    spread = vol[:, None]
    dist_now = dist_prev + (0.03 - 0.5 * spread * spread) + spread * shock
    crossing = jnp.exp(
        -2.0 * jnp.maximum(dist_prev, 0.0) * jnp.maximum(dist_now, 0.0) / (spread * spread)
    )
    losses = jnp.sum(jnp.maximum(net_value, 0.0) * crossing, axis=1)
    tile = jnp.broadcast_to(jnp.pad(losses, (0, LANES - owned)), (8, LANES))
    summed = jnp.sum(everywhere(tile, "scen").reshape(-1, 8, LANES)[:, 0, :owned], axis=0)
    expected_loss = summed / (scen_rows * lax.axis_size("scen"))
    return (net_value, expected_loss)


def solution(mesh):
    chips = Mesh(mesh.devices.reshape(4, 8, 2, 8), ("x", "y", "core", "scen"))
    in_specs = (
        P("scen", TRADE, None),
        P(TRADE, None),
        P(TRADE),
        P(None, TRADE),
        P(TRADE),
        P(TRADE),
        P(TRADE, "scen"),
        P(TRADE, "scen"),
        P(TRADE),
    )
    out_specs = (P(TRADE, "scen"), P(TRADE))
    return jax.shard_map(body, mesh=chips, in_specs=in_specs, out_specs=out_specs, check_vma=False)
```

```python
import jax
import jax.numpy as jnp
from jax import lax
from jax.experimental import pallas as pl
from jax.experimental.pallas import tpu as pltpu
from jax.sharding import Mesh, PartitionSpec as P

LANES = 128
HINT = 25 * 10**8
LIMIT = 16
PACK_LIMIT = 62
TRADE = ("x", "y", "core")


def shift(value, axis, by):
    size = lax.axis_size(axis)
    return lax.ppermute(value, axis, [(i, (i + by) % size) for i in range(size)])


def everywhere(value, axis):
    size = lax.axis_size(axis)
    copies = jnp.broadcast_to(value[None], (size, *value.shape))
    return lax.all_to_all(copies, axis, 0, 0, tiled=True)


def pack_kernel(
    live_ref, cash_hbm, id_hbm, yield_hbm, load_hbm, draw_hbm, out_hbm, half_hbm, copies_hbm,
    cash_ref, load_ref, draw_ref, fold_ref, id_ref, yield_ref, sems
):
    pillars, trades = cash_ref.shape
    width = load_hbm.shape[1]
    rows = fold_ref.shape[0]
    set_total = width * rows // pillars
    yield_in = pltpu.make_async_copy(yield_hbm, yield_ref, sems.at[5])
    yield_in.start()
    id_in = pltpu.make_async_copy(id_hbm, id_ref, sems.at[6])
    id_in.start()
    cash_in = pltpu.make_async_copy(cash_hbm, cash_ref, sems.at[0])
    cash_in.start()
    draw_in = pltpu.make_async_copy(draw_hbm.at[0], draw_ref, sems.at[1])
    draw_in.start()
    load_in = pltpu.make_async_copy(load_hbm, load_ref.at[:, pl.ds(0, width)], sems.at[2])
    load_in.start()
    yield_in.wait()
    diagonal = lax.broadcasted_iota(jnp.int32, (pillars, pillars), 0) == lax.broadcasted_iota(
        jnp.int32, (pillars, pillars), 1
    )
    level = jnp.sum(jnp.where(diagonal, yield_ref[...], 0.0), axis=1, keepdims=True)
    upper = level.astype(jnp.bfloat16).astype(jnp.float32)
    middle = (level - upper).astype(jnp.bfloat16).astype(jnp.float32)
    lower = level - upper - middle
    lane = lax.broadcasted_iota(jnp.int32, (pillars, LANES), 1)
    terms = jnp.where(
        lane == 0, upper, jnp.where(lane == 1, middle, jnp.where(lane == 2, lower, 0.0))
    )
    load_ref[:, width:] = terms.astype(jnp.bfloat16)
    id_in.wait()
    alive = lax.broadcasted_iota(jnp.int32, (1, trades), 1) < live_ref[0]
    owner = jnp.where(alive, id_ref[...], -1)
    fold_ref[:, width:] = jnp.zeros((rows, LANES), jnp.bfloat16)
    draw_in.wait()
    moves = [
        pltpu.make_async_copy(draw_ref, copies_hbm.at[i], sems.at[9 + i])
        for i in range(copies_hbm.shape[0])
    ]
    for move in moves:
        move.start()
    cash_in.wait()
    load_in.wait()
    load_out = pltpu.make_async_copy(load_ref, out_hbm.at[pl.ds(0, pillars)], sems.at[3])
    load_out.start()
    start = pl.multiple_of(lax.rem(lax.axis_index("scen"), 2) * (width // 2), LANES)
    span = half_hbm.shape[1]
    load_half = pltpu.make_async_copy(
        load_ref.at[:, pl.ds(start, span)], half_hbm.at[pl.ds(0, pillars)], sems.at[7]
    )
    load_half.start()
    for first in range(0, set_total, 256):
        numbers = first + lax.broadcasted_iota(jnp.int32, (256, trades), 0)
        member = jnp.where(numbers == owner, 1.0, 0.0).astype(jnp.bfloat16)
        flows = lax.dot_general(
            cash_ref[...], member, (((1,), (1,)), ((), ())), preferred_element_type=jnp.float32
        ).astype(jnp.bfloat16)
        for i in range(pillars // rows):
            fold_ref[:, i * set_total + first : i * set_total + first + 256] = flows[
                i * rows : (i + 1) * rows
            ]
    fold_out = pltpu.make_async_copy(fold_ref, out_hbm.at[pl.ds(pillars, rows)], sems.at[4])
    fold_out.start()
    fold_half = pltpu.make_async_copy(
        fold_ref.at[:, pl.ds(start, span)], half_hbm.at[pl.ds(pillars, rows)], sems.at[8]
    )
    fold_half.start()
    load_half.wait()
    fold_half.wait()
    load_out.wait()
    fold_out.wait()
    for move in moves:
        move.wait()


def discounts(pack_ref, pillars, normals_ref):
    width = normals_ref.shape[1]
    factors = lax.dot_general(
        pack_ref[:pillars, :width],
        normals_ref[...],
        (((1,), (1,)), ((), ())),
        preferred_element_type=jnp.float32,
    )
    step = (lax.broadcasted_iota(jnp.int32, (pillars, 1), 0) + 1).astype(jnp.float32)
    level = jnp.sum(pack_ref[:pillars, width:].astype(jnp.float32), axis=1, keepdims=True)
    return jnp.exp(-step * (16.0 / pillars) * (level + 0.02 * factors)).astype(jnp.bfloat16)


def unfold(pack_ref, pillars, set_total):
    rows = pack_ref.shape[0] - pillars
    return jnp.concatenate(
        [
            pack_ref[pillars:, i * set_total : (i + 1) * set_total]
            for i in range(pillars // rows)
        ],
        axis=0,
    )


def join_kernel(near_half, next_half, out_ref):
    middle = out_ref.shape[1] - near_half.shape[1]
    even = lax.rem(lax.axis_index("scen"), 2) == 0

    def join(low_ref, high_ref):
        out_ref[:, :middle] = low_ref[:, :middle]
        out_ref[:, middle:] = high_ref[...]

    @pl.when(even)
    def _():
        join(near_half, next_half)

    @pl.when(jnp.logical_not(even))
    def _():
        join(next_half, near_half)


def values(pack_refs, pillars, set_total, normals_ref):
    return lax.dot_general(
        jnp.concatenate([unfold(ref, pillars, set_total) for ref in pack_refs], axis=0),
        jnp.concatenate([discounts(ref, pillars, normals_ref) for ref in pack_refs], axis=0),
        (((0,), (0,)), ((), ())),
        preferred_element_type=jnp.float32,
    )


def first_kernel(mine_ref, other_ref, own_ref, far_ref, normals_ref, total_ref):
    set_total = total_ref.shape[0]
    width = normals_ref.shape[1]
    pillars = own_ref.shape[0] * width // (width + set_total)
    rows = mine_ref.shape[1]
    first = lax.axis_index("core") == 0

    def place(even_ref, odd_ref):
        for i in range(mine_ref.shape[0]):
            normals_ref[2 * i * rows : 2 * (i + 1) * rows, :] = jnp.concatenate(
                [even_ref[i], odd_ref[i]], axis=0
            )

    @pl.when(first)
    def _():
        place(mine_ref, other_ref)

    @pl.when(jnp.logical_not(first))
    def _():
        place(other_ref, mine_ref)

    total_ref[...] = values([own_ref, far_ref], pillars, set_total, normals_ref)


def price_kernel(normals_ref, total_ref, *refs):
    pack_refs, out_ref = refs[:-1], refs[-1]
    set_total = out_ref.shape[0]
    width = normals_ref.shape[1]
    pillars = pack_refs[0].shape[0] * width // (width + set_total)
    rest = values(pack_refs, pillars, set_total, normals_ref)
    out_ref[...] = (total_ref[...] + rest).astype(jnp.bfloat16)


def body(draws, loadings, base_yield, cashflows, netting_id, live_trades, dist_prev, shock, vol):
    pillars = loadings.shape[0]
    owned, scen_rows = dist_prev.shape
    quarters = lax.axis_size("x")
    groups = quarters * lax.axis_size("y") * lax.axis_size("core")
    set_total = owned * groups
    part = scen_rows // quarters
    width = loadings.shape[1]
    rows = pillars * set_total // width
    vmem = pl.BlockSpec(memory_space=pltpu.VMEM)
    hbm = pl.BlockSpec(memory_space=pltpu.HBM)
    smem = pl.BlockSpec(memory_space=pltpu.SMEM)
    params = pltpu.CompilerParams(vmem_limit_bytes=LIMIT << 20)

    packed, half, copies = pl.pallas_call(
        pack_kernel,
        out_shape=(
            jax.ShapeDtypeStruct((pillars + rows, width + LANES), jnp.bfloat16),
            jax.ShapeDtypeStruct((pillars + rows, width // 2 + LANES), jnp.bfloat16),
            jax.ShapeDtypeStruct((lax.axis_size("y"), *draws.shape[1:]), jnp.bfloat16),
        ),
        in_specs=[smem, hbm, hbm, hbm, hbm, hbm],
        out_specs=(hbm, hbm, hbm),
        scratch_shapes=[
            pltpu.VMEM(cashflows.shape, jnp.bfloat16),
            pltpu.VMEM((pillars, width + LANES), jnp.bfloat16),
            pltpu.VMEM(draws.shape[1:], jnp.bfloat16),
            pltpu.VMEM((rows, width + LANES), jnp.bfloat16),
            pltpu.VMEM((1, netting_id.shape[0]), jnp.int32),
            pltpu.VMEM((1, pillars), jnp.float32),
            pltpu.SemaphoreType.DMA((9 + lax.axis_size("y"),)),
        ],
        compiler_params=pltpu.CompilerParams(vmem_limit_bytes=PACK_LIMIT << 20),
        name="pack",
    )(live_trades, cashflows, netting_id[None, :], base_yield[None, :], loadings, draws)
    packs = [shift(packed, "x", by) for by in (1, -1)]
    far = shift(half, "x", 2)
    planes = lax.axis_size("scen")
    rest = lax.ppermute(far, "scen", [(i, i ^ 1) for i in range(planes)])
    mine = lax.all_to_all(copies, "y", 0, 0, tiled=True)
    other = shift(mine, "core", 1)
    joined = pl.pallas_call(
        join_kernel,
        out_shape=jax.ShapeDtypeStruct(packed.shape, packed.dtype),
        in_specs=[vmem, vmem],
        out_specs=vmem,
        compiler_params=params,
        cost_estimate=pl.CostEstimate(flops=HINT, bytes_accessed=0, transcendentals=0),
        name="join",
    )(far, rest)
    normals, total = pl.pallas_call(
        first_kernel,
        out_shape=(
            jax.ShapeDtypeStruct((part, width), jnp.bfloat16),
            jax.ShapeDtypeStruct((set_total, part), jnp.float32),
        ),
        in_specs=[vmem] * 4,
        out_specs=(vmem, vmem),
        compiler_params=params,
        cost_estimate=pl.CostEstimate(flops=0, bytes_accessed=0, transcendentals=0),
        name="first",
    )(mine, other, packed, joined)
    total = pl.pallas_call(
        price_kernel,
        out_shape=jax.ShapeDtypeStruct((set_total, part), jnp.bfloat16),
        in_specs=[vmem] * 4,
        out_specs=vmem,
        compiler_params=params,
        name="price",
    )(normals, total, *packs)
    sent = lax.all_to_all(total, TRADE, 0, 0, tiled=True)
    terms = sent.reshape(quarters, groups // quarters, owned, part).astype(jnp.float32)
    net_value = jnp.sum(terms, axis=1).transpose(1, 0, 2).reshape(owned, scen_rows)

    spread = vol[:, None]
    dist_now = dist_prev + (0.03 - 0.5 * spread * spread) + spread * shock
    crossing = jnp.exp(
        -2.0 * jnp.maximum(dist_prev, 0.0) * jnp.maximum(dist_now, 0.0) / (spread * spread)
    )
    losses = jnp.sum(jnp.maximum(net_value, 0.0) * crossing, axis=1)
    tile = jnp.broadcast_to(jnp.pad(losses, (0, LANES - owned)), (8, LANES))
    summed = jnp.sum(everywhere(tile, "scen").reshape(-1, 8, LANES)[:, 0, :owned], axis=0)
    expected_loss = summed / (scen_rows * lax.axis_size("scen"))
    return (net_value, expected_loss)


def solution(mesh):
    chips = Mesh(mesh.devices.reshape(4, 8, 2, 8), ("x", "y", "core", "scen"))
    in_specs = (
        P("scen", TRADE, None),
        P(TRADE, None),
        P(TRADE),
        P(None, TRADE),
        P(TRADE),
        P(TRADE),
        P(TRADE, "scen"),
        P(TRADE, "scen"),
        P(TRADE),
    )
    out_specs = (P(TRADE, "scen"), P(TRADE))
    return jax.shard_map(body, mesh=chips, in_specs=in_specs, out_specs=out_specs, check_vma=False)
```

```python
import jax
import jax.numpy as jnp
from jax import lax
from jax.experimental import pallas as pl
from jax.experimental.pallas import tpu as pltpu
from jax.sharding import Mesh, PartitionSpec as P

LANES = 128
HINT = 25 * 10**8
LIMIT = 16
PACK_LIMIT = 62
TRADE = ("x", "y", "core")


def shift(value, axis, by):
    size = lax.axis_size(axis)
    return lax.ppermute(value, axis, [(i, (i + by) % size) for i in range(size)])


def everywhere(value, axis):
    size = lax.axis_size(axis)
    copies = jnp.broadcast_to(value[None], (size, *value.shape))
    return lax.all_to_all(copies, axis, 0, 0, tiled=True)


def pack_kernel(
    live_ref, cash_hbm, id_hbm, yield_hbm, load_hbm, draw_hbm, out_hbm, half_hbm, copies_hbm,
    cash_ref, load_ref, draw_ref, fold_ref, id_ref, yield_ref, sems
):
    pillars, trades = cash_ref.shape
    width = load_hbm.shape[1]
    rows = fold_ref.shape[0]
    set_total = width * rows // pillars
    yield_in = pltpu.make_async_copy(yield_hbm, yield_ref, sems.at[5])
    yield_in.start()
    id_in = pltpu.make_async_copy(id_hbm, id_ref, sems.at[6])
    id_in.start()
    cash_in = pltpu.make_async_copy(cash_hbm, cash_ref, sems.at[0])
    cash_in.start()
    draw_in = pltpu.make_async_copy(draw_hbm.at[0], draw_ref, sems.at[1])
    draw_in.start()
    load_in = pltpu.make_async_copy(load_hbm, load_ref.at[:, pl.ds(0, width)], sems.at[2])
    load_in.start()
    yield_in.wait()
    diagonal = lax.broadcasted_iota(jnp.int32, (pillars, pillars), 0) == lax.broadcasted_iota(
        jnp.int32, (pillars, pillars), 1
    )
    level = jnp.sum(jnp.where(diagonal, yield_ref[...], 0.0), axis=1, keepdims=True)
    upper = level.astype(jnp.bfloat16).astype(jnp.float32)
    middle = (level - upper).astype(jnp.bfloat16).astype(jnp.float32)
    lower = level - upper - middle
    lane = lax.broadcasted_iota(jnp.int32, (pillars, LANES), 1)
    terms = jnp.where(
        lane == 0, upper, jnp.where(lane == 1, middle, jnp.where(lane == 2, lower, 0.0))
    )
    load_ref[:, width:] = terms.astype(jnp.bfloat16)
    id_in.wait()
    alive = lax.broadcasted_iota(jnp.int32, (1, trades), 1) < live_ref[0]
    owner = jnp.where(alive, id_ref[...], -1)
    fold_ref[:, width:] = jnp.zeros((rows, LANES), jnp.bfloat16)
    draw_in.wait()
    moves = [
        pltpu.make_async_copy(draw_ref, copies_hbm.at[i], sems.at[9 + i])
        for i in range(copies_hbm.shape[0])
    ]
    for move in moves:
        move.start()
    cash_in.wait()
    load_in.wait()
    load_out = pltpu.make_async_copy(load_ref, out_hbm.at[pl.ds(0, pillars)], sems.at[3])
    load_out.start()
    start = pl.multiple_of(lax.rem(lax.axis_index("scen"), 2) * (width // 2), LANES)
    span = half_hbm.shape[1]
    load_half = pltpu.make_async_copy(
        load_ref.at[:, pl.ds(start, span)], half_hbm.at[pl.ds(0, pillars)], sems.at[7]
    )
    load_half.start()
    for first in range(0, set_total, 256):
        numbers = first + lax.broadcasted_iota(jnp.int32, (256, trades), 0)
        member = jnp.where(numbers == owner, 1.0, 0.0).astype(jnp.bfloat16)
        flows = lax.dot_general(
            cash_ref[...], member, (((1,), (1,)), ((), ())), preferred_element_type=jnp.float32
        ).astype(jnp.bfloat16)
        for i in range(pillars // rows):
            fold_ref[:, i * set_total + first : i * set_total + first + 256] = flows[
                i * rows : (i + 1) * rows
            ]
    fold_out = pltpu.make_async_copy(fold_ref, out_hbm.at[pl.ds(pillars, rows)], sems.at[4])
    fold_out.start()
    fold_half = pltpu.make_async_copy(
        fold_ref.at[:, pl.ds(start, span)], half_hbm.at[pl.ds(pillars, rows)], sems.at[8]
    )
    fold_half.start()
    load_half.wait()
    fold_half.wait()
    load_out.wait()
    fold_out.wait()
    for move in moves:
        move.wait()


def discounts(pack_ref, pillars, normals_ref):
    width = normals_ref.shape[1]
    factors = lax.dot_general(
        pack_ref[:pillars, :width],
        normals_ref[...],
        (((1,), (1,)), ((), ())),
        preferred_element_type=jnp.float32,
    )
    step = (lax.broadcasted_iota(jnp.int32, (pillars, 1), 0) + 1).astype(jnp.float32)
    level = jnp.sum(pack_ref[:pillars, width:].astype(jnp.float32), axis=1, keepdims=True)
    return jnp.exp(-step * (16.0 / pillars) * (level + 0.02 * factors)).astype(jnp.bfloat16)


def unfold(pack_ref, pillars, set_total):
    rows = pack_ref.shape[0] - pillars
    return jnp.concatenate(
        [
            pack_ref[pillars:, i * set_total : (i + 1) * set_total]
            for i in range(pillars // rows)
        ],
        axis=0,
    )


def join_kernel(near_half, next_half, out_ref):
    middle = out_ref.shape[1] - near_half.shape[1]
    even = lax.rem(lax.axis_index("scen"), 2) == 0

    def join(low_ref, high_ref):
        out_ref[:, :middle] = low_ref[:, :middle]
        out_ref[:, middle:] = high_ref[...]

    @pl.when(even)
    def _():
        join(near_half, next_half)

    @pl.when(jnp.logical_not(even))
    def _():
        join(next_half, near_half)


def values(pack_refs, pillars, set_total, normals_ref):
    return lax.dot_general(
        jnp.concatenate([unfold(ref, pillars, set_total) for ref in pack_refs], axis=0),
        jnp.concatenate([discounts(ref, pillars, normals_ref) for ref in pack_refs], axis=0),
        (((0,), (0,)), ((), ())),
        preferred_element_type=jnp.float32,
    )


def first_kernel(
    mine_ref, other_ref, own_ref, far_ref, dist_ref, shock_ref, vol_ref,
    normals_ref, total_ref, crossing_ref
):
    owned = dist_ref.shape[0]
    diagonal = lax.broadcasted_iota(jnp.int32, (owned, owned), 0) == lax.broadcasted_iota(
        jnp.int32, (owned, owned), 1
    )
    spread = jnp.sum(jnp.where(diagonal, vol_ref[...], 0.0), axis=1, keepdims=True)
    dist_prev = dist_ref[...]
    dist_now = dist_prev + (0.03 - 0.5 * spread * spread) + spread * shock_ref[...]
    crossing_ref[...] = jnp.exp(
        -2.0 * jnp.maximum(dist_prev, 0.0) * jnp.maximum(dist_now, 0.0) / (spread * spread)
    )
    set_total = total_ref.shape[0]
    width = normals_ref.shape[1]
    pillars = own_ref.shape[0] * width // (width + set_total)
    rows = mine_ref.shape[1]
    first = lax.axis_index("core") == 0

    def place(even_ref, odd_ref):
        for i in range(mine_ref.shape[0]):
            normals_ref[2 * i * rows : 2 * (i + 1) * rows, :] = jnp.concatenate(
                [even_ref[i], odd_ref[i]], axis=0
            )

    @pl.when(first)
    def _():
        place(mine_ref, other_ref)

    @pl.when(jnp.logical_not(first))
    def _():
        place(other_ref, mine_ref)

    total_ref[...] = values([own_ref, far_ref], pillars, set_total, normals_ref)


def price_kernel(normals_ref, total_ref, *refs):
    pack_refs, out_ref = refs[:-1], refs[-1]
    set_total = out_ref.shape[0]
    width = normals_ref.shape[1]
    pillars = pack_refs[0].shape[0] * width // (width + set_total)
    rest = values(pack_refs, pillars, set_total, normals_ref)
    out_ref[...] = (total_ref[...] + rest).astype(jnp.bfloat16)


def body(draws, loadings, base_yield, cashflows, netting_id, live_trades, dist_prev, shock, vol):
    pillars = loadings.shape[0]
    owned, scen_rows = dist_prev.shape
    quarters = lax.axis_size("x")
    groups = quarters * lax.axis_size("y") * lax.axis_size("core")
    set_total = owned * groups
    part = scen_rows // quarters
    width = loadings.shape[1]
    rows = pillars * set_total // width
    vmem = pl.BlockSpec(memory_space=pltpu.VMEM)
    hbm = pl.BlockSpec(memory_space=pltpu.HBM)
    smem = pl.BlockSpec(memory_space=pltpu.SMEM)
    params = pltpu.CompilerParams(vmem_limit_bytes=LIMIT << 20)

    packed, half, copies = pl.pallas_call(
        pack_kernel,
        out_shape=(
            jax.ShapeDtypeStruct((pillars + rows, width + LANES), jnp.bfloat16),
            jax.ShapeDtypeStruct((pillars + rows, width // 2 + LANES), jnp.bfloat16),
            jax.ShapeDtypeStruct((lax.axis_size("y"), *draws.shape[1:]), jnp.bfloat16),
        ),
        in_specs=[smem, hbm, hbm, hbm, hbm, hbm],
        out_specs=(hbm, hbm, hbm),
        scratch_shapes=[
            pltpu.VMEM(cashflows.shape, jnp.bfloat16),
            pltpu.VMEM((pillars, width + LANES), jnp.bfloat16),
            pltpu.VMEM(draws.shape[1:], jnp.bfloat16),
            pltpu.VMEM((rows, width + LANES), jnp.bfloat16),
            pltpu.VMEM((1, netting_id.shape[0]), jnp.int32),
            pltpu.VMEM((1, pillars), jnp.float32),
            pltpu.SemaphoreType.DMA((9 + lax.axis_size("y"),)),
        ],
        compiler_params=pltpu.CompilerParams(vmem_limit_bytes=PACK_LIMIT << 20),
        name="pack",
    )(live_trades, cashflows, netting_id[None, :], base_yield[None, :], loadings, draws)
    packs = [shift(packed, "x", by) for by in (1, -1)]
    far = shift(half, "x", 2)
    planes = lax.axis_size("scen")
    rest = lax.ppermute(far, "scen", [(i, i ^ 1) for i in range(planes)])
    mine = lax.all_to_all(copies, "y", 0, 0, tiled=True)
    other = shift(mine, "core", 1)
    joined = pl.pallas_call(
        join_kernel,
        out_shape=jax.ShapeDtypeStruct(packed.shape, packed.dtype),
        in_specs=[vmem, vmem],
        out_specs=vmem,
        compiler_params=params,
        cost_estimate=pl.CostEstimate(flops=HINT, bytes_accessed=0, transcendentals=0),
        name="join",
    )(far, rest)
    normals, total, crossing = pl.pallas_call(
        first_kernel,
        out_shape=(
            jax.ShapeDtypeStruct((part, width), jnp.bfloat16),
            jax.ShapeDtypeStruct((set_total, part), jnp.float32),
            jax.ShapeDtypeStruct(dist_prev.shape, jnp.float32),
        ),
        in_specs=[vmem] * 7,
        out_specs=(vmem, vmem, vmem),
        compiler_params=params,
        cost_estimate=pl.CostEstimate(flops=0, bytes_accessed=0, transcendentals=0),
        name="first",
    )(mine, other, packed, joined, dist_prev, shock, vol[None, :])
    total = pl.pallas_call(
        price_kernel,
        out_shape=jax.ShapeDtypeStruct((set_total, part), jnp.bfloat16),
        in_specs=[vmem] * 4,
        out_specs=vmem,
        compiler_params=params,
        name="price",
    )(normals, total, *packs)
    sent = lax.all_to_all(total, TRADE, 0, 0, tiled=True)
    terms = sent.reshape(quarters, groups // quarters, owned, part).astype(jnp.float32)
    net_value = jnp.sum(terms, axis=1).transpose(1, 0, 2).reshape(owned, scen_rows)

    losses = jnp.sum(jnp.maximum(net_value, 0.0) * crossing, axis=1)
    tile = jnp.broadcast_to(jnp.pad(losses, (0, LANES - owned)), (8, LANES))
    summed = jnp.sum(everywhere(tile, "scen").reshape(-1, 8, LANES)[:, 0, :owned], axis=0)
    expected_loss = summed / (scen_rows * lax.axis_size("scen"))
    return (net_value, expected_loss)


def solution(mesh):
    chips = Mesh(mesh.devices.reshape(4, 8, 2, 8), ("x", "y", "core", "scen"))
    in_specs = (
        P("scen", TRADE, None),
        P(TRADE, None),
        P(TRADE),
        P(None, TRADE),
        P(TRADE),
        P(TRADE),
        P(TRADE, "scen"),
        P(TRADE, "scen"),
        P(TRADE),
    )
    out_specs = (P(TRADE, "scen"), P(TRADE))
    return jax.shard_map(body, mesh=chips, in_specs=in_specs, out_specs=out_specs, check_vma=False)
```

```python
import jax
import jax.numpy as jnp
from jax import lax
from jax.experimental import pallas as pl
from jax.experimental.pallas import tpu as pltpu
from jax.sharding import Mesh, PartitionSpec as P

LANES = 128
HOLD = 8 * 10**9
HINT = 25 * 10**8
LIMIT = 16
PACK_LIMIT = 62
TRADE = ("x", "y", "core")


def shift(value, axis, by):
    size = lax.axis_size(axis)
    return lax.ppermute(value, axis, [(i, (i + by) % size) for i in range(size)])


def everywhere(value, axis):
    size = lax.axis_size(axis)
    copies = jnp.broadcast_to(value[None], (size, *value.shape))
    return lax.all_to_all(copies, axis, 0, 0, tiled=True)


def pack_kernel(
    live_ref, cash_hbm, id_hbm, yield_hbm, load_hbm, draw_hbm, out_hbm, half_hbm, copies_hbm,
    cash_ref, load_ref, draw_ref, fold_ref, id_ref, yield_ref, sems
):
    pillars, trades = cash_ref.shape
    width = load_hbm.shape[1]
    rows = fold_ref.shape[0]
    set_total = width * rows // pillars
    yield_in = pltpu.make_async_copy(yield_hbm, yield_ref, sems.at[5])
    yield_in.start()
    id_in = pltpu.make_async_copy(id_hbm, id_ref, sems.at[6])
    id_in.start()
    cash_in = pltpu.make_async_copy(cash_hbm, cash_ref, sems.at[0])
    cash_in.start()
    draw_in = pltpu.make_async_copy(draw_hbm.at[0], draw_ref, sems.at[1])
    draw_in.start()
    load_in = pltpu.make_async_copy(load_hbm, load_ref.at[:, pl.ds(0, width)], sems.at[2])
    load_in.start()
    yield_in.wait()
    diagonal = lax.broadcasted_iota(jnp.int32, (pillars, pillars), 0) == lax.broadcasted_iota(
        jnp.int32, (pillars, pillars), 1
    )
    level = jnp.sum(jnp.where(diagonal, yield_ref[...], 0.0), axis=1, keepdims=True)
    upper = level.astype(jnp.bfloat16).astype(jnp.float32)
    middle = (level - upper).astype(jnp.bfloat16).astype(jnp.float32)
    lower = level - upper - middle
    lane = lax.broadcasted_iota(jnp.int32, (pillars, LANES), 1)
    terms = jnp.where(
        lane == 0, upper, jnp.where(lane == 1, middle, jnp.where(lane == 2, lower, 0.0))
    )
    load_ref[:, width:] = terms.astype(jnp.bfloat16)
    id_in.wait()
    alive = lax.broadcasted_iota(jnp.int32, (1, trades), 1) < live_ref[0]
    owner = jnp.where(alive, id_ref[...], -1)
    fold_ref[:, width:] = jnp.zeros((rows, LANES), jnp.bfloat16)
    draw_in.wait()
    moves = [
        pltpu.make_async_copy(draw_ref, copies_hbm.at[i], sems.at[9 + i])
        for i in range(copies_hbm.shape[0])
    ]
    for move in moves:
        move.start()
    def members(first):
        numbers = first + lax.broadcasted_iota(jnp.int32, (256, trades), 0)
        return jnp.where(numbers == owner, 1.0, 0.0).astype(jnp.bfloat16)

    member = members(0)
    cash_in.wait()
    load_in.wait()
    load_out = pltpu.make_async_copy(load_ref, out_hbm.at[pl.ds(0, pillars)], sems.at[3])
    load_out.start()
    start = pl.multiple_of(lax.rem(lax.axis_index("scen"), 2) * (width // 2), LANES)
    span = half_hbm.shape[1]
    load_half = pltpu.make_async_copy(
        load_ref.at[:, pl.ds(start, span)], half_hbm.at[pl.ds(0, pillars)], sems.at[7]
    )
    load_half.start()
    for first in range(0, set_total, 256):
        if first > 0:
            member = members(first)
        flows = lax.dot_general(
            cash_ref[...], member, (((1,), (1,)), ((), ())), preferred_element_type=jnp.float32
        ).astype(jnp.bfloat16)
        for i in range(pillars // rows):
            fold_ref[:, i * set_total + first : i * set_total + first + 256] = flows[
                i * rows : (i + 1) * rows
            ]
    fold_out = pltpu.make_async_copy(fold_ref, out_hbm.at[pl.ds(pillars, rows)], sems.at[4])
    fold_out.start()
    fold_half = pltpu.make_async_copy(
        fold_ref.at[:, pl.ds(start, span)], half_hbm.at[pl.ds(pillars, rows)], sems.at[8]
    )
    fold_half.start()
    load_half.wait()
    fold_half.wait()
    load_out.wait()
    fold_out.wait()
    for move in moves:
        move.wait()


def discounts(pack_ref, pillars, normals_ref):
    width = normals_ref.shape[1]
    factors = lax.dot_general(
        pack_ref[:pillars, :width],
        normals_ref[...],
        (((1,), (1,)), ((), ())),
        preferred_element_type=jnp.float32,
    )
    step = (lax.broadcasted_iota(jnp.int32, (pillars, 1), 0) + 1).astype(jnp.float32)
    level = jnp.sum(pack_ref[:pillars, width:].astype(jnp.float32), axis=1, keepdims=True)
    return jnp.exp(-step * (16.0 / pillars) * (level + 0.02 * factors)).astype(jnp.bfloat16)


def unfold(pack_ref, pillars, set_total):
    rows = pack_ref.shape[0] - pillars
    return jnp.concatenate(
        [
            pack_ref[pillars:, i * set_total : (i + 1) * set_total]
            for i in range(pillars // rows)
        ],
        axis=0,
    )


def hold_kernel(half_ref, out_ref):
    del half_ref
    out_ref[...] = jnp.zeros_like(out_ref)


def join_kernel(
    near_half, next_half, held_ref, dist_ref, shock_ref, vol_ref, out_ref, crossing_ref
):
    del held_ref
    owned = dist_ref.shape[0]
    diagonal = lax.broadcasted_iota(jnp.int32, (owned, owned), 0) == lax.broadcasted_iota(
        jnp.int32, (owned, owned), 1
    )
    spread = jnp.sum(jnp.where(diagonal, vol_ref[...], 0.0), axis=1, keepdims=True)
    dist_prev = dist_ref[...]
    dist_now = dist_prev + (0.03 - 0.5 * spread * spread) + spread * shock_ref[...]
    crossing_ref[...] = jnp.exp(
        -2.0 * jnp.maximum(dist_prev, 0.0) * jnp.maximum(dist_now, 0.0) / (spread * spread)
    )
    middle = out_ref.shape[1] - near_half.shape[1]
    even = lax.rem(lax.axis_index("scen"), 2) == 0

    def join(low_ref, high_ref):
        out_ref[:, :middle] = low_ref[:, :middle]
        out_ref[:, middle:] = high_ref[...]

    @pl.when(even)
    def _():
        join(near_half, next_half)

    @pl.when(jnp.logical_not(even))
    def _():
        join(next_half, near_half)


def values(pack_refs, pillars, set_total, normals_ref):
    return lax.dot_general(
        jnp.concatenate([unfold(ref, pillars, set_total) for ref in pack_refs], axis=0),
        jnp.concatenate([discounts(ref, pillars, normals_ref) for ref in pack_refs], axis=0),
        (((0,), (0,)), ((), ())),
        preferred_element_type=jnp.float32,
    )


def first_kernel(
    mine_ref, other_ref, own_ref, far_ref, normals_ref, total_ref
):
    set_total = total_ref.shape[0]
    width = normals_ref.shape[1]
    pillars = own_ref.shape[0] * width // (width + set_total)
    rows = mine_ref.shape[1]
    first = lax.axis_index("core") == 0

    def place(even_ref, odd_ref):
        for i in range(mine_ref.shape[0]):
            normals_ref[2 * i * rows : 2 * (i + 1) * rows, :] = jnp.concatenate(
                [even_ref[i], odd_ref[i]], axis=0
            )

    @pl.when(first)
    def _():
        place(mine_ref, other_ref)

    @pl.when(jnp.logical_not(first))
    def _():
        place(other_ref, mine_ref)

    total_ref[...] = values([own_ref, far_ref], pillars, set_total, normals_ref)


def price_kernel(normals_ref, total_ref, *refs):
    pack_refs, out_ref = refs[:-1], refs[-1]
    set_total = out_ref.shape[0]
    width = normals_ref.shape[1]
    pillars = pack_refs[0].shape[0] * width // (width + set_total)
    rest = values(pack_refs, pillars, set_total, normals_ref)
    out_ref[...] = (total_ref[...] + rest).astype(jnp.bfloat16)


def body(draws, loadings, base_yield, cashflows, netting_id, live_trades, dist_prev, shock, vol):
    pillars = loadings.shape[0]
    owned, scen_rows = dist_prev.shape
    quarters = lax.axis_size("x")
    groups = quarters * lax.axis_size("y") * lax.axis_size("core")
    set_total = owned * groups
    part = scen_rows // quarters
    width = loadings.shape[1]
    rows = pillars * set_total // width
    vmem = pl.BlockSpec(memory_space=pltpu.VMEM)
    hbm = pl.BlockSpec(memory_space=pltpu.HBM)
    smem = pl.BlockSpec(memory_space=pltpu.SMEM)
    params = pltpu.CompilerParams(vmem_limit_bytes=LIMIT << 20)

    packed, half, copies = pl.pallas_call(
        pack_kernel,
        out_shape=(
            jax.ShapeDtypeStruct((pillars + rows, width + LANES), jnp.bfloat16),
            jax.ShapeDtypeStruct((pillars + rows, width // 2 + LANES), jnp.bfloat16),
            jax.ShapeDtypeStruct((lax.axis_size("y"), *draws.shape[1:]), jnp.bfloat16),
        ),
        in_specs=[smem, hbm, hbm, hbm, hbm, hbm],
        out_specs=(hbm, hbm, hbm),
        scratch_shapes=[
            pltpu.VMEM(cashflows.shape, jnp.bfloat16),
            pltpu.VMEM((pillars, width + LANES), jnp.bfloat16),
            pltpu.VMEM(draws.shape[1:], jnp.bfloat16),
            pltpu.VMEM((rows, width + LANES), jnp.bfloat16),
            pltpu.VMEM((1, netting_id.shape[0]), jnp.int32),
            pltpu.VMEM((1, pillars), jnp.float32),
            pltpu.SemaphoreType.DMA((9 + lax.axis_size("y"),)),
        ],
        compiler_params=pltpu.CompilerParams(vmem_limit_bytes=PACK_LIMIT << 20),
        name="pack",
    )(live_trades, cashflows, netting_id[None, :], base_yield[None, :], loadings, draws)
    packs = [shift(packed, "x", by) for by in (1, -1)]
    far = shift(half, "x", 2)
    held = pl.pallas_call(
        hold_kernel,
        out_shape=jax.ShapeDtypeStruct((8, LANES), jnp.float32),
        in_specs=[pl.BlockSpec(memory_space=pl.ANY)],
        out_specs=vmem,
        compiler_params=params,
        cost_estimate=pl.CostEstimate(flops=HOLD, bytes_accessed=0, transcendentals=0),
        name="hold",
    )(far)
    far, held = lax.optimization_barrier((far, held))
    planes = lax.axis_size("scen")
    rest = lax.ppermute(far, "scen", [(i, i ^ 1) for i in range(planes)])
    mine = lax.all_to_all(copies, "y", 0, 0, tiled=True)
    other = shift(mine, "core", 1)
    joined, crossing = pl.pallas_call(
        join_kernel,
        out_shape=(
            jax.ShapeDtypeStruct(packed.shape, packed.dtype),
            jax.ShapeDtypeStruct(dist_prev.shape, jnp.float32),
        ),
        in_specs=[vmem] * 6,
        out_specs=(vmem, vmem),
        compiler_params=params,
        cost_estimate=pl.CostEstimate(flops=HINT, bytes_accessed=0, transcendentals=0),
        name="join",
    )(far, rest, held, dist_prev, shock, vol[None, :])
    normals, total = pl.pallas_call(
        first_kernel,
        out_shape=(
            jax.ShapeDtypeStruct((part, width), jnp.bfloat16),
            jax.ShapeDtypeStruct((set_total, part), jnp.float32),
        ),
        in_specs=[vmem] * 4,
        out_specs=(vmem, vmem),
        compiler_params=params,
        cost_estimate=pl.CostEstimate(flops=0, bytes_accessed=0, transcendentals=0),
        name="first",
    )(mine, other, packed, joined)
    total = pl.pallas_call(
        price_kernel,
        out_shape=jax.ShapeDtypeStruct((set_total, part), jnp.bfloat16),
        in_specs=[vmem] * 4,
        out_specs=vmem,
        compiler_params=params,
        name="price",
    )(normals, total, *packs)
    sent = lax.all_to_all(total, TRADE, 0, 0, tiled=True)
    terms = sent.reshape(quarters, groups // quarters, owned, part).astype(jnp.float32)
    net_value = jnp.sum(terms, axis=1).transpose(1, 0, 2).reshape(owned, scen_rows)

    losses = jnp.sum(jnp.maximum(net_value, 0.0) * crossing, axis=1)
    tile = jnp.pad(losses, (0, LANES - owned))[None]
    summed = jnp.sum(everywhere(tile, "scen").reshape(-1, LANES)[:, :owned], axis=0)
    expected_loss = summed / (scen_rows * lax.axis_size("scen"))
    return (net_value, expected_loss)


def solution(mesh):
    chips = Mesh(mesh.devices.reshape(4, 8, 2, 8), ("x", "y", "core", "scen"))
    in_specs = (
        P("scen", TRADE, None),
        P(TRADE, None),
        P(TRADE),
        P(None, TRADE),
        P(TRADE),
        P(TRADE),
        P(TRADE, "scen"),
        P(TRADE, "scen"),
        P(TRADE),
    )
    out_specs = (P(TRADE, "scen"), P(TRADE))
    return jax.shard_map(body, mesh=chips, in_specs=in_specs, out_specs=out_specs, check_vma=False)
```
